768 devices in a mesh: sub: 96 (over z, x, core), grp: 8 (over y).
Axes of the slice: x: 4, y: 8, z: 12, core: 2. Of those that a mesh axis runs over, the one named last changes fastest.
Arguments:
- basis: bfloat16 [1536, 64, 4096], P(('sub', 'grp')), may hold values from -3 to 3
- stiffness: bfloat16 [6144, 4, 128, 128], P(('sub', 'grp')), may hold values from -0.5 to 0.5
- pair_subs: int32 [6144, 2], P(('sub', 'grp')), may hold values from 0 to 1
- own_rows: int32 [6144, 4], P(('sub', 'grp')), may hold values from 0 to 31, as said below
- far_rows: int32 [6144, 4], P(('sub', 'grp')), may hold values from 0 to 31, as said below
- pair_count: int32 [768], P(('sub', 'grp')), may hold values from 1 to 8, as said below
Outputs:
- owned_blocks: float32 [6144, 4096], P('sub')
- partner_blocks: float32 [6144, 4096], P('sub')
The draws below stay inside these ranges and needn't reach their ends.
Inputs may be any that keep to these rules, and one draw needn't show every extreme that they name: `own_rows`: the 4 tiles of one pair are distinct. `far_rows`: the 4 tiles of one pair are distinct. `pair_count`: live slots are the first ones of a device; some device has all 8 live in every draw.
All inputs are finite; a program needn't handle non-finite values.
Results may differ from the reference program's by a relative error of at most 0.0029.
Values may be sent and summed in bfloat16 or wider, within the bound.
No kernel may reach another device: no remote copies, remote signals or barrier semaphores. Data moves between devices by JAX's collectives and lax.ppermute only.
A program may use at most 32 MiB of HBM per device.

```python
import jax
import jax.numpy as jnp
from jax import lax

NB = 64
LOC = 4096
SUB_DEV = 2
PAIR_DEV = 8
TILES = 4
PAIRS = 6144
SUBS = 1536
N_SUB = 96
N_GRP = 8


def distinct_tiles(key):
    scores = jax.random.randint(key, (PAIRS, LOC // 128), 0, 1073741824)
    order = jnp.argsort(scores, axis=1, stable=True)
    return order[:, :TILES].astype(jnp.int32)


def draw_own_rows(key, part):
    key = jax.random.fold_in(key, 11)
    return distinct_tiles(key)


def draw_far_rows(key, part):
    key = jax.random.fold_in(key, 23)
    return distinct_tiles(key)


def draw_pair_count(key, part):
    key = jax.random.fold_in(key, 37)
    first_key, second_key = jax.random.split(key)
    counts = jax.random.randint(first_key, (N_SUB * N_GRP,), PAIR_DEV // 2, PAIR_DEV + 1)
    fullest = jax.random.randint(second_key, (), 0, N_SUB * N_GRP)
    return counts.at[fullest].set(PAIR_DEV).astype(jnp.int32)


def place_ends(values, own_key, low, high):
    place = [jax.random.randint(jax.random.fold_in(own_key, axis), (), 0, length) for axis, length in enumerate(values.shape)]
    widest = values.shape.index(max(values.shape))
    next_to = place[:widest] + [(place[widest] + 1) % values.shape[widest]] + place[widest + 1:]
    return values.at[tuple(place)].set(low).at[tuple(next_to)].set(high)


def block_scale(key, shape, pieces, smallest, top_value):
    gain, own = 1.0, jax.random.fold_in(key, 6)
    for axis_at, blocks in pieces:
        heights = jnp.exp(jax.random.uniform(jax.random.fold_in(own, axis_at), (blocks,), jnp.float32, smallest / len(pieces), top_value / len(pieces)))
        gain = gain * jnp.repeat(heights, shape[axis_at] // blocks).reshape([-1 if axis == axis_at else 1 for axis in range(len(shape))])
    return gain


def bell_draw(rng, dims, width, reach, cuts=(), held_as=jnp.bfloat16):
    loudness = block_scale(rng, dims, cuts, -0.22, 0.18) if cuts else 1.0
    entries = jax.random.normal(rng, dims, jnp.float32) * width * loudness
    return jnp.minimum(jnp.maximum(entries, -reach), reach).astype(held_as)


def setup_inputs(seed: int = 0) -> dict:
    splits = jax.random.split(jax.random.key(seed), 7)
    basis = bell_draw(splits[0], (SUBS, NB, LOC), (1.0 / (TILES * 128) ** 0.25), 3.0, ((0, 768),))
    stiffness = bell_draw(splits[1], (PAIRS, TILES, 128, 128), 128 ** -0.5, 0.5, ((0, 768),))
    pair_subs = place_ends(jax.random.randint(splits[2], (PAIRS, 2), 0, SUB_DEV), jax.random.fold_in(splits[2], 1), 0, SUB_DEV - 1).astype(jnp.int32)
    own_rows = draw_own_rows(jax.random.fold_in(splits[6], 71), 0)
    far_rows = draw_far_rows(jax.random.fold_in(splits[6], 71), 0)
    pair_count = draw_pair_count(jax.random.fold_in(splits[6], 71), 0)
    return {"basis": basis, "stiffness": stiffness, "pair_subs": pair_subs, "own_rows": own_rows, "far_rows": far_rows, "pair_count": pair_count}


def collect(basis_block, sub_choice, margin_tiles):
    basis_width, local_total = basis_block.shape[1], basis_block.shape[2]
    tiled = basis_block.reshape(basis_block.shape[0], basis_width, local_total // 128, 128)

    def one_pair(s, tiles):
        picked = jnp.take(tiled[s], tiles, axis=1)
        return picked.reshape(basis_width, tiles.shape[0] * 128)

    return jax.vmap(one_pair)(sub_choice, margin_tiles)


def cross_blocks(own_part, far_part, stiff_tiles, live_count):
    pair_total, basis_width, margin_total = far_part.shape
    tile_count = stiff_tiles.shape[1]
    far_tiles = far_part.reshape(pair_total, basis_width, tile_count, margin_total // tile_count).astype(jnp.float32)
    stiff_image = jnp.einsum("pntc,ptrc->pntr", far_tiles, stiff_tiles.astype(jnp.float32)).astype(jnp.bfloat16)
    stiff_image = stiff_image.reshape(pair_total, basis_width, margin_total)
    blocks = jnp.einsum("pno,pmo->pnm", own_part.astype(jnp.float32), stiff_image.astype(jnp.float32))
    keep_mask = (jnp.arange(pair_total, dtype=jnp.int32) < live_count).astype(jnp.float32)
    return blocks * keep_mask[:, None, None]


def reference(basis, stiffness, pair_subs, own_rows, far_rows, pair_count):
    device_total = N_SUB * N_GRP
    grouped = basis.reshape(device_total, SUB_DEV, NB, LOC)
    stiff_all = stiffness.reshape(device_total, PAIR_DEV, TILES, 128, 128)
    sub_all = pair_subs.reshape(device_total, PAIR_DEV, 2)
    own_all = own_rows.reshape(device_total, PAIR_DEV, TILES)
    far_all = far_rows.reshape(device_total, PAIR_DEV, TILES)

    def one_device(device):
        i = device // N_GRP
        g = device % N_GRP
        partner = ((i + N_SUB - 1) % N_SUB) * N_GRP + g
        own_part = collect(grouped[device], sub_all[device][:, 0], own_all[device])
        far_part = collect(grouped[partner], sub_all[device][:, 1], far_all[device])
        return cross_blocks(own_part, far_part, stiff_all[device], pair_count[device])

    blocks = lax.map(one_device, jnp.arange(device_total, dtype=jnp.int32))
    owned_blocks = blocks.reshape(PAIRS, NB * NB)
    following = jnp.roll(blocks.reshape(N_SUB, N_GRP, PAIR_DEV, NB, NB), -1, axis=0)
    partner_blocks = jnp.swapaxes(following, -1, -2).reshape(PAIRS, NB * NB)
    return (owned_blocks, partner_blocks)
```

```python
import jax
import jax.numpy as jnp
from jax import lax
from jax.experimental import pallas as pl
from jax.experimental.pallas import tpu as pltpu
from jax.sharding import PartitionSpec as P

VMEM_LIMIT = 16 * 1024 * 1024


def shifted(block, axis, distance):
    devices = range(lax.axis_size(axis))
    route = [((i - distance) % len(devices), i) for i in devices]
    return lax.ppermute(block, axis, route)


def collect_kernel(wanted_ref, basis_ref, part_ref, sems):
    pair_total, tile_count = wanted_ref.shape
    tile_total = basis_ref.shape[2] // 128
    copies = []
    for p in range(pair_total):
        for t in range(tile_count):
            code = wanted_ref[p, t]
            s = code // tile_total
            first = pl.multiple_of((code - s * tile_total) * 128, 128)
            copy = pltpu.make_async_copy(
                basis_ref.at[s, :, pl.ds(first, 128)],
                part_ref.at[p, :, pl.ds(t * 128, 128)],
                sems.at[p, t],
            )
            copy.start()
            copies.append(copy)
    for copy in copies:
        copy.wait()


def collect(basis, wanted):
    pair_total, tile_count = wanted.shape
    shape = (pair_total, basis.shape[1], tile_count * 128)
    return pl.pallas_call(
        collect_kernel,
        out_shape=jax.ShapeDtypeStruct(shape, basis.dtype),
        in_specs=[
            pl.BlockSpec(memory_space=pltpu.SMEM),
            pl.BlockSpec(memory_space=pl.ANY),
        ],
        out_specs=pl.BlockSpec(memory_space=pl.ANY),
        scratch_shapes=[pltpu.SemaphoreType.DMA((pair_total, tile_count))],
        compiler_params=pltpu.CompilerParams(vmem_limit_bytes=VMEM_LIMIT),
        cost_estimate=pl.CostEstimate(flops=0, bytes_accessed=2**20, transcendentals=0),
        name="collect",
    )(wanted, basis)


def flat_rows(rows_ref, width):
    left = lax.broadcasted_iota(jnp.int32, (8, 2 * width), 1) < width
    for k in range(width // 2):
        even = rows_ref[pl.ds(2 * k, 8, stride=width), :]
        odd = rows_ref[pl.ds(2 * k + 1, 8, stride=width), :]
        yield k, jnp.where(left, even, odd)


NT = (((1,), (1,)), ((), ()))


def cross_kernel(count_ref, own_ref, far_ref, stiff_ref, out_ref, rows_ref):
    pair_total, width, _ = far_ref.shape
    tile_count = stiff_ref.shape[1]
    live = count_ref[0]
    for p in range(pair_total):
        image = jnp.concatenate(
            [
                lax.dot_general(
                    far_ref[p, :, t * 128 : (t + 1) * 128],
                    stiff_ref[p, t],
                    NT,
                    preferred_element_type=jnp.float32,
                ).astype(jnp.bfloat16)
                for t in range(tile_count)
            ],
            axis=1,
        )
        own = own_ref[p]
        flipped = lax.dot_general(
            image,
            jnp.concatenate([own, own], axis=0),
            NT,
            preferred_element_type=jnp.float32,
        )
        rows_ref[p * width : (p + 1) * width, :] = jnp.where(p < live, flipped, 0.0)
    for k, row in flat_rows(rows_ref, width):
        row = row.astype(out_ref.dtype)
        for d in range(out_ref.shape[0]):
            out_ref[d, :, 2 * width * k : 2 * width * (k + 1)] = row


def cross_blocks(live, own_part, far_part, stiffness, copies):
    pair_total, width, _ = far_part.shape
    vmem = pl.BlockSpec(memory_space=pltpu.VMEM)
    return pl.pallas_call(
        cross_kernel,
        out_shape=jax.ShapeDtypeStruct((copies, pair_total, width * width), jnp.bfloat16),
        in_specs=[pl.BlockSpec(memory_space=pltpu.SMEM), vmem, vmem, vmem],
        out_specs=vmem,
        scratch_shapes=[pltpu.VMEM((pair_total * width, 2 * width), jnp.float32)],
        compiler_params=pltpu.CompilerParams(vmem_limit_bytes=VMEM_LIMIT),
        cost_estimate=pl.CostEstimate(flops=2**27, bytes_accessed=2**21, transcendentals=0),
        name="cross_blocks",
    )(live, own_part, far_part, stiffness)


def turn_kernel(flat_ref, out_ref, split_ref, rows_ref):
    group_total, pair_total, flat_width = flat_ref.shape
    width = rows_ref.shape[1] // 2
    row_at = lax.broadcasted_iota(jnp.int32, (width, 2 * width), 0)
    lane_at = lax.broadcasted_iota(jnp.int32, (width, 2 * width), 1)
    pick = (row_at == lane_at).astype(jnp.bfloat16)

    @pl.loop(0, group_total)
    def _(g):
        for k in range(width // 2):
            both = flat_ref[g, :, 2 * width * k : 2 * width * (k + 1)].astype(jnp.float32)
            split_ref[pl.ds(2 * k, 8, stride=width), :] = both
            split_ref[pl.ds(2 * k + 1, 8, stride=width), :] = pltpu.roll(both, width, 1)
        for p in range(pair_total):
            matrix = split_ref[p * width : (p + 1) * width, :].astype(jnp.bfloat16)
            rows_ref[p * width : (p + 1) * width, :] = lax.dot_general(
                pick,
                jnp.concatenate([matrix, matrix], axis=0),
                NT,
                preferred_element_type=jnp.float32,
            )
        first = pl.multiple_of(g * pair_total, pair_total)
        for k, row in flat_rows(rows_ref, width):
            out_ref[pl.ds(first, pair_total), 2 * width * k : 2 * width * (k + 1)] = row


def turned(flat, width):
    group_total, pair_total, flat_width = flat.shape
    vmem = pl.BlockSpec(memory_space=pltpu.VMEM)
    scratch = pltpu.VMEM((pair_total * width, 2 * width), jnp.float32)
    return pl.pallas_call(
        turn_kernel,
        out_shape=jax.ShapeDtypeStruct((group_total * pair_total, flat_width), jnp.float32),
        in_specs=[vmem],
        out_specs=vmem,
        scratch_shapes=[scratch, scratch],
        compiler_params=pltpu.CompilerParams(vmem_limit_bytes=VMEM_LIMIT),
        cost_estimate=pl.CostEstimate(flops=2**27, bytes_accessed=2**21, transcendentals=0),
        name="turned",
    )(flat)


def on_device(basis, stiffness, pair_subs, own_rows, far_rows, pair_count):
    tile_total = basis.shape[2] // 128
    width = basis.shape[1]
    wanted = shifted(far_rows + pair_subs[:, 1:2] * tile_total, "sub", -1)
    own_part = collect(basis, own_rows + pair_subs[:, 0:1] * tile_total)
    far_part = shifted(collect(basis, wanted), "sub", 1)
    groups = lax.axis_size("grp")
    flipped = cross_blocks(pair_count, own_part, far_part, stiffness, groups)
    gathered = lax.all_to_all(flipped, "grp", 0, 0)
    returned = shifted(gathered, "sub", -1)
    owned_all = turned(gathered, width)
    partner_all = returned.reshape(owned_all.shape).astype(jnp.float32)
    return (owned_all, partner_all)


def solution(mesh):
    return jax.shard_map(
        on_device,
        mesh=mesh,
        in_specs=(
            P(("sub", "grp"), None, None),
            P(("sub", "grp"), None, None, None),
            P(("sub", "grp"), None),
            P(("sub", "grp"), None),
            P(("sub", "grp"), None),
            P(("sub", "grp")),
        ),
        out_specs=(P("sub", None), P("sub", None)),
        check_vma=False,
    )
```

```python
import jax
import jax.numpy as jnp
from jax import lax
from jax.experimental import pallas as pl
from jax.experimental.pallas import tpu as pltpu
from jax.sharding import PartitionSpec as P

VMEM_LIMIT = 16 * 1024 * 1024


def shifted(block, axis, distance):
    devices = range(lax.axis_size(axis))
    route = [((i - distance) % len(devices), i) for i in devices]
    return lax.ppermute(block, axis, route)


NT = (((1,), (1,)), ((), ()))
PITCH = 72


def flat_rows(rows_ref, width):
    left = lax.broadcasted_iota(jnp.int32, (8, 2 * width), 1) < width
    for k in range(width // 2):
        even = rows_ref[pl.ds(2 * k, 8, stride=PITCH), :]
        odd = rows_ref[pl.ds(2 * k + 1, 8, stride=PITCH), :]
        yield k, jnp.where(left, even, odd)


OWN_SUB, FAR_SUB, OWN_TILES, FAR_TILES, LIVE = 0, 1, 2, 6, 10


def planned(pair_subs, own_rows, far_rows, pair_count):
    pair_total = own_rows.shape[0]
    live = jnp.broadcast_to(pair_count[:, None], (1, pair_total))
    return jnp.concatenate([pair_subs.T, own_rows.T, far_rows.T, live], axis=0)


def tile(basis_ref, plan_ref, sub_at, tile_at, p):
    first = pl.multiple_of(plan_ref[tile_at, p] * 128, 128)
    return basis_ref[plan_ref[sub_at, p], :, pl.ds(first, 128)]


def collect_kernel(plan_ref, basis_ref, part_ref):
    pair_total, _, margin = part_ref.shape
    for p in range(pair_total):
        for t in range(margin // 128):
            part_ref[p, :, t * 128 : (t + 1) * 128] = tile(
                basis_ref, plan_ref, OWN_SUB, OWN_TILES + t, p
            )


def collect(plan, basis, tile_count):
    vmem = pl.BlockSpec(memory_space=pltpu.VMEM)
    shape = (plan.shape[1], basis.shape[1], tile_count * 128)
    return pl.pallas_call(
        collect_kernel,
        out_shape=jax.ShapeDtypeStruct(shape, basis.dtype),
        in_specs=[pl.BlockSpec(memory_space=pltpu.SMEM), vmem],
        out_specs=vmem,
        compiler_params=pltpu.CompilerParams(vmem_limit_bytes=VMEM_LIMIT),
        cost_estimate=pl.CostEstimate(flops=2**27, bytes_accessed=2**22, transcendentals=0),
        name="collect",
    )(plan, basis)


def cross_kernel(plan_ref, own_ref, far_ref, stiff_ref, out_ref, rows_ref):
    pair_total, tile_count = stiff_ref.shape[:2]
    width = far_ref.shape[1]

    def imaged(p):
        return jnp.concatenate(
            [
                lax.dot_general(
                    tile(far_ref, plan_ref, FAR_SUB, FAR_TILES + t, p),
                    stiff_ref[p, t],
                    NT,
                    preferred_element_type=jnp.float32,
                ).astype(jnp.bfloat16)
                for t in range(tile_count)
            ],
            axis=1,
        )

    def crossed(p, image):
        own = own_ref[p]
        flipped = lax.dot_general(
            image,
            jnp.concatenate([own, own], axis=0),
            NT,
            preferred_element_type=jnp.float32,
        )
        keep = p < plan_ref[LIVE, p]
        rows_ref[p * PITCH : p * PITCH + width, :] = jnp.where(keep, flipped, 0.0)

    image = imaged(0)
    for p in range(pair_total):
        later = imaged(p + 1) if p + 1 < pair_total else None
        crossed(p, image)
        image = later
    for k, row in flat_rows(rows_ref, width):
        row = row.astype(out_ref.dtype)
        for d in range(out_ref.shape[0]):
            out_ref[d, :, 2 * width * k : 2 * width * (k + 1)] = row


def cross_blocks(plan, own_part, far_basis, stiffness, copies):
    pair_total, width, _ = own_part.shape
    vmem = pl.BlockSpec(memory_space=pltpu.VMEM)
    return pl.pallas_call(
        cross_kernel,
        out_shape=jax.ShapeDtypeStruct((copies, pair_total, width * width), jnp.bfloat16),
        in_specs=[pl.BlockSpec(memory_space=pltpu.SMEM), vmem, vmem, vmem],
        out_specs=vmem,
        scratch_shapes=[pltpu.VMEM((pair_total * PITCH, 2 * width), jnp.float32)],
        compiler_params=pltpu.CompilerParams(vmem_limit_bytes=VMEM_LIMIT),
        cost_estimate=pl.CostEstimate(flops=2**27, bytes_accessed=2**21, transcendentals=0),
        name="cross_blocks",
    )(plan, own_part, far_basis, stiffness)


ORDER = [5, 4, 6, 3, 7, 2, 0, 1]


def rows_copy(held_ref, out_ref, sems, g):
    pair_total = held_ref.shape[1]
    first = ORDER[g] * pair_total
    return pltpu.make_async_copy(
        held_ref.at[g], out_ref.at[pl.ds(first, pair_total), :], sems.at[g]
    )


LANES = 4


def turn_kernel(flat_ref, out_ref, held_ref, sems, *scratch):
    group_total, pair_total, _ = flat_ref.shape
    width = scratch[0].shape[1] // 2
    row_at = lax.broadcasted_iota(jnp.int32, (width, 2 * width), 0)
    lane_at = lax.broadcasted_iota(jnp.int32, (width, 2 * width), 1)
    pick = (row_at == lane_at).astype(jnp.bfloat16)

    for g in range(group_total):
        split_ref, rows_ref = scratch[2 * (g % LANES) : 2 * (g % LANES) + 2]
        for k in range(width // 2):
            both = flat_ref[g, :, 2 * width * k : 2 * width * (k + 1)].astype(jnp.float32)
            split_ref[pl.ds(2 * k, 8, stride=PITCH), :] = both
            split_ref[pl.ds(2 * k + 1, 8, stride=PITCH), :] = pltpu.roll(both, width, 1)
        for p in range(pair_total):
            here = slice(p * PITCH, p * PITCH + width)
            matrix = split_ref[here, :].astype(jnp.bfloat16)
            rows_ref[here, :] = lax.dot_general(
                pick,
                jnp.concatenate([matrix, matrix], axis=0),
                NT,
                preferred_element_type=jnp.float32,
            )
        for k, row in flat_rows(rows_ref, width):
            held_ref[g, :, 2 * width * k : 2 * width * (k + 1)] = row
        rows_copy(held_ref, out_ref, sems, g).start()

    for g in range(group_total):
        rows_copy(held_ref, out_ref, sems, g).wait()


def widen_kernel(flat_ref, out_ref, held_ref, sems):
    group_total = flat_ref.shape[0]
    for g in range(group_total):
        held_ref[g] = flat_ref[g].astype(jnp.float32)
        rows_copy(held_ref, out_ref, sems, g).start()
    for g in range(group_total):
        rows_copy(held_ref, out_ref, sems, g).wait()


def spread(kernel, name, flat, scratch):
    group_total, pair_total, flat_width = flat.shape
    return pl.pallas_call(
        kernel,
        out_shape=jax.ShapeDtypeStruct((group_total * pair_total, flat_width), jnp.float32),
        in_specs=[pl.BlockSpec(memory_space=pltpu.VMEM)],
        out_specs=pl.BlockSpec(memory_space=pl.ANY),
        scratch_shapes=[
            pltpu.VMEM(flat.shape, jnp.float32),
            pltpu.SemaphoreType.DMA((group_total,)),
            *scratch,
        ],
        compiler_params=pltpu.CompilerParams(vmem_limit_bytes=VMEM_LIMIT),
        cost_estimate=pl.CostEstimate(flops=2**27, bytes_accessed=2**21, transcendentals=0),
        name=name,
    )(flat)


def on_device(basis, stiffness, pair_subs, own_rows, far_rows, pair_count):
    width = basis.shape[1]
    pair_total, tile_count = own_rows.shape
    far_basis = shifted(basis, "sub", 1)
    plan = planned(pair_subs, own_rows, far_rows, pair_count)
    own_part = collect(plan, basis, tile_count)
    flipped = cross_blocks(plan, own_part, far_basis, stiffness, lax.axis_size("grp"))
    gathered = lax.all_to_all(flipped, "grp", 0, 0, axis_index_groups=[ORDER])
    returned = shifted(gathered, "sub", -1)
    block_rows = pltpu.VMEM((pair_total * PITCH, 2 * width), jnp.float32)
    owned_all = spread(turn_kernel, "turned", gathered, [block_rows] * (2 * LANES))
    partner_all = spread(widen_kernel, "widened", returned, [])
    return (owned_all, partner_all)


def solution(mesh):
    return jax.shard_map(
        on_device,
        mesh=mesh,
        in_specs=(
            P(("sub", "grp"), None, None),
            P(("sub", "grp"), None, None, None),
            P(("sub", "grp"), None),
            P(("sub", "grp"), None),
            P(("sub", "grp"), None),
            P(("sub", "grp")),
        ),
        out_specs=(P("sub", None), P("sub", None)),
        check_vma=False,
    )
```

```python
import jax
import jax.numpy as jnp
from jax import lax
from jax.experimental import pallas as pl
from jax.experimental.pallas import tpu as pltpu
from jax.sharding import PartitionSpec as P

VMEM_LIMIT = 16 * 1024 * 1024


def shifted(block, axis, distance):
    devices = range(lax.axis_size(axis))
    route = [((i - distance) % len(devices), i) for i in devices]
    return lax.ppermute(block, axis, route)


NT = (((1,), (1,)), ((), ()))
PITCH = 72


def block_rows(pair_total, width):
    return pltpu.VMEM(((pair_total + 1) * PITCH, 2 * width), jnp.float32)


def flat_rows(rows_ref, width):
    left = lax.broadcasted_iota(jnp.int32, (8, 2 * width), 1) < width
    for k in range(width // 2):
        even = rows_ref[pl.ds(2 * k, 8, stride=PITCH), :]
        odd = rows_ref[pl.ds(2 * k + 1, 8, stride=PITCH), :]
        yield k, jnp.where(left, even, odd)


OWN_SUB, FAR_SUB, OWN_TILES, FAR_TILES, LIVE = 0, 1, 2, 6, 10
PAIRS = 8


def planned(pair_subs, own_rows, far_rows, pair_count):
    pair_total = own_rows.shape[0]
    live = jnp.broadcast_to(pair_count[:, None], (1, pair_total))
    return jnp.concatenate([pair_subs.T, own_rows.T, far_rows.T, live], axis=0).reshape(-1)


def tile(basis_ref, plan_ref, sub_at, tile_at, p):
    first = pl.multiple_of(plan_ref[tile_at * PAIRS + p] * 128, 128)
    return basis_ref[plan_ref[sub_at * PAIRS + p], :, pl.ds(first, 128)]


def collect_kernel(plan_ref, basis_ref, part_ref):
    pair_total, _, margin = part_ref.shape
    for p in range(pair_total):
        for t in range(margin // 128):
            part_ref[p, :, t * 128 : (t + 1) * 128] = tile(
                basis_ref, plan_ref, OWN_SUB, OWN_TILES + t, p
            )


def collect(plan, basis, tile_count):
    vmem = pl.BlockSpec(memory_space=pltpu.VMEM)
    shape = (PAIRS, basis.shape[1], tile_count * 128)
    return pl.pallas_call(
        collect_kernel,
        out_shape=jax.ShapeDtypeStruct(shape, basis.dtype),
        in_specs=[pl.BlockSpec(memory_space=pltpu.SMEM), vmem],
        out_specs=vmem,
        compiler_params=pltpu.CompilerParams(vmem_limit_bytes=VMEM_LIMIT),
        cost_estimate=pl.CostEstimate(flops=2**27, bytes_accessed=2**22, transcendentals=0),
        name="collect",
    )(plan, basis)


def cross_kernel(plan_ref, own_ref, far_ref, stiff_ref, out_ref, rows_ref):
    pair_total, tile_count = stiff_ref.shape[:2]
    width = far_ref.shape[1]

    def imaged(p):
        return jnp.concatenate(
            [
                lax.dot_general(
                    tile(far_ref, plan_ref, FAR_SUB, FAR_TILES + t, p),
                    stiff_ref[p, t],
                    NT,
                    preferred_element_type=jnp.float32,
                ).astype(jnp.bfloat16)
                for t in range(tile_count)
            ],
            axis=1,
        )

    def crossed(p, image):
        own = own_ref[p]
        flipped = lax.dot_general(
            image,
            jnp.concatenate([own, own], axis=0),
            NT,
            preferred_element_type=jnp.float32,
        )
        keep = p < plan_ref[LIVE * PAIRS + p]
        rows_ref[p * PITCH : p * PITCH + width, :] = jnp.where(keep, flipped, 0.0)

    image = imaged(0)
    for p in range(pair_total):
        later = imaged(p + 1) if p + 1 < pair_total else None
        crossed(p, image)
        image = later
    for k, row in flat_rows(rows_ref, width):
        row = row.astype(out_ref.dtype)
        for d in range(out_ref.shape[0]):
            out_ref[d, :, 2 * width * k : 2 * width * (k + 1)] = row


def cross_blocks(plan, own_part, far_basis, stiffness, copies):
    pair_total, width, _ = own_part.shape
    vmem = pl.BlockSpec(memory_space=pltpu.VMEM)
    return pl.pallas_call(
        cross_kernel,
        out_shape=jax.ShapeDtypeStruct((copies, pair_total, width * width), jnp.bfloat16),
        in_specs=[pl.BlockSpec(memory_space=pltpu.SMEM), vmem, vmem, vmem],
        out_specs=vmem,
        scratch_shapes=[block_rows(pair_total, width)],
        compiler_params=pltpu.CompilerParams(vmem_limit_bytes=VMEM_LIMIT),
        cost_estimate=pl.CostEstimate(flops=2**27, bytes_accessed=2**21, transcendentals=0),
        name="cross_blocks",
    )(plan, own_part, far_basis, stiffness)


ORDER = [5, 4, 6, 3, 7, 2, 0, 1]


def rows_copy(held_ref, out_ref, sems, g):
    pair_total = held_ref.shape[1]
    first = ORDER[g] * pair_total
    return pltpu.make_async_copy(
        held_ref.at[g], out_ref.at[pl.ds(first, pair_total), :], sems.at[g]
    )


LANES = 4


def turn_kernel(flat_ref, out_ref, held_ref, sems, *scratch):
    group_total, pair_total, _ = flat_ref.shape
    width = scratch[0].shape[1] // 2
    row_at = lax.broadcasted_iota(jnp.int32, (width, 2 * width), 0)
    lane_at = lax.broadcasted_iota(jnp.int32, (width, 2 * width), 1)
    pick = (row_at == lane_at).astype(jnp.bfloat16)

    for g in range(group_total):
        split_ref, rows_ref = scratch[2 * (g % LANES) : 2 * (g % LANES) + 2]
        for k in range(width // 2):
            both = flat_ref[g, :, 2 * width * k : 2 * width * (k + 1)].astype(jnp.float32)
            split_ref[pl.ds(2 * k, 8, stride=PITCH), :] = both
            split_ref[pl.ds(2 * k + 1, 8, stride=PITCH), :] = pltpu.roll(both, width, 1)
        for p in range(pair_total):
            here = slice(p * PITCH, p * PITCH + width)
            matrix = split_ref[here, :].astype(jnp.bfloat16)
            rows_ref[here, :] = lax.dot_general(
                pick,
                jnp.concatenate([matrix, matrix], axis=0),
                NT,
                preferred_element_type=jnp.float32,
            )
        for k, row in flat_rows(rows_ref, width):
            held_ref[g, :, 2 * width * k : 2 * width * (k + 1)] = row
        rows_copy(held_ref, out_ref, sems, g).start()

    for g in range(group_total):
        rows_copy(held_ref, out_ref, sems, g).wait()


def widen_kernel(flat_ref, out_ref, held_ref, sems):
    group_total = flat_ref.shape[0]
    for g in range(group_total):
        held_ref[g] = flat_ref[g].astype(jnp.float32)
        rows_copy(held_ref, out_ref, sems, g).start()
    for g in range(group_total):
        rows_copy(held_ref, out_ref, sems, g).wait()


def spread(kernel, name, flat, scratch):
    group_total, pair_total, flat_width = flat.shape
    return pl.pallas_call(
        kernel,
        out_shape=jax.ShapeDtypeStruct((group_total * pair_total, flat_width), jnp.float32),
        in_specs=[pl.BlockSpec(memory_space=pltpu.VMEM)],
        out_specs=pl.BlockSpec(memory_space=pl.ANY),
        scratch_shapes=[
            pltpu.VMEM(flat.shape, jnp.float32),
            pltpu.SemaphoreType.DMA((group_total,)),
            *scratch,
        ],
        compiler_params=pltpu.CompilerParams(vmem_limit_bytes=VMEM_LIMIT),
        cost_estimate=pl.CostEstimate(flops=2**27, bytes_accessed=2**21, transcendentals=0),
        name=name,
    )(flat)


def on_device(basis, stiffness, pair_subs, own_rows, far_rows, pair_count):
    width = basis.shape[1]
    pair_total, tile_count = own_rows.shape
    far_basis = shifted(basis, "sub", 1)
    plan = planned(pair_subs, own_rows, far_rows, pair_count)
    own_part = collect(plan, basis, tile_count)
    flipped = cross_blocks(plan, own_part, far_basis, stiffness, lax.axis_size("grp"))
    gathered = lax.all_to_all(flipped, "grp", 0, 0, axis_index_groups=[ORDER])
    returned = shifted(gathered, "sub", -1)
    block_scratch = [block_rows(pair_total, width)] * (2 * LANES)
    owned_all = spread(turn_kernel, "turned", gathered, block_scratch)
    partner_all = spread(widen_kernel, "widened", returned, [])
    return (owned_all, partner_all)


def solution(mesh):
    return jax.shard_map(
        on_device,
        mesh=mesh,
        in_specs=(
            P(("sub", "grp"), None, None),
            P(("sub", "grp"), None, None, None),
            P(("sub", "grp"), None),
            P(("sub", "grp"), None),
            P(("sub", "grp"), None),
            P(("sub", "grp")),
        ),
        out_specs=(P("sub", None), P("sub", None)),
        check_vma=False,
    )
```

```python
import jax
import jax.numpy as jnp
from jax import lax
from jax.experimental import pallas as pl
from jax.experimental.pallas import tpu as pltpu
from jax.sharding import PartitionSpec as P

VMEM_LIMIT = 16 * 1024 * 1024


def shifted(block, axis, distance):
    devices = range(lax.axis_size(axis))
    route = [((i - distance) % len(devices), i) for i in devices]
    return lax.ppermute(block, axis, route)


NT = (((1,), (1,)), ((), ()))
PITCH = 72


def block_rows(pair_total, width):
    return pltpu.VMEM(((pair_total + 1) * PITCH, 2 * width), jnp.float32)


def flat_row(rows_ref, width, k):
    left = lax.broadcasted_iota(jnp.int32, (8, 2 * width), 1) < width
    even = rows_ref[pl.ds(2 * k, 8, stride=PITCH), :]
    odd = rows_ref[pl.ds(2 * k + 1, 8, stride=PITCH), :]
    return jnp.where(left, even, odd)


OWN_SUB, FAR_SUB, OWN_TILES, FAR_TILES, LIVE = 0, 1, 2, 6, 10
PAIRS = 8


def planned(pair_subs, own_rows, far_rows, pair_count):
    pair_total = own_rows.shape[0]
    live = jnp.broadcast_to(pair_count[:, None], (1, pair_total))
    return jnp.concatenate([pair_subs.T, own_rows.T, far_rows.T, live], axis=0).reshape(-1)


def tile(basis_ref, plan_ref, sub_at, tile_at, p):
    first = pl.multiple_of(plan_ref[tile_at * PAIRS + p] * 128, 128)
    return basis_ref[plan_ref[sub_at * PAIRS + p], :, pl.ds(first, 128)]


def collect_kernel(plan_ref, basis_ref, part_ref):
    pair_total, _, margin = part_ref.shape
    for p in range(pair_total):
        for t in range(margin // 128):
            part_ref[p, :, t * 128 : (t + 1) * 128] = tile(
                basis_ref, plan_ref, OWN_SUB, OWN_TILES + t, p
            )


def collect(plan, basis, tile_count):
    vmem = pl.BlockSpec(memory_space=pltpu.VMEM)
    shape = (PAIRS, basis.shape[1], tile_count * 128)
    return pl.pallas_call(
        collect_kernel,
        out_shape=jax.ShapeDtypeStruct(shape, basis.dtype),
        in_specs=[pl.BlockSpec(memory_space=pltpu.SMEM), vmem],
        out_specs=vmem,
        compiler_params=pltpu.CompilerParams(vmem_limit_bytes=VMEM_LIMIT),
        cost_estimate=pl.CostEstimate(flops=2**27, bytes_accessed=2**22, transcendentals=0),
        name="collect",
    )(plan, basis)


def cross_kernel(plan_ref, own_ref, far_ref, stiff_ref, out_ref, rows_ref):
    pair_total, tile_count = stiff_ref.shape[:2]
    width = far_ref.shape[1]

    def imaged(p):
        return jnp.concatenate(
            [
                lax.dot_general(
                    tile(far_ref, plan_ref, FAR_SUB, FAR_TILES + t, p),
                    stiff_ref[p, t],
                    NT,
                    preferred_element_type=jnp.float32,
                ).astype(jnp.bfloat16)
                for t in range(tile_count)
            ],
            axis=1,
        )

    def crossed(p, image):
        own = own_ref[p]
        flipped = lax.dot_general(
            image,
            jnp.concatenate([own, own], axis=0),
            NT,
            preferred_element_type=jnp.float32,
        )
        keep = p < plan_ref[LIVE * PAIRS + p]
        rows_ref[p * PITCH : p * PITCH + width, :] = jnp.where(keep, flipped, 0.0)

    image = imaged(0)
    for p in range(pair_total):
        later = imaged(p + 1) if p + 1 < pair_total else None
        crossed(p, image)
        image = later
    half = width // 4
    for k in range(half):
        both = [flat_row(rows_ref, width, k), flat_row(rows_ref, width, k + half)]
        row = jnp.concatenate(both, axis=0).astype(out_ref.dtype)
        for d in range(out_ref.shape[0]):
            out_ref[d, :, 2 * width * k : 2 * width * (k + 1)] = row


def cross_blocks(plan, own_part, far_basis, stiffness, copies):
    pair_total, width, _ = own_part.shape
    vmem = pl.BlockSpec(memory_space=pltpu.VMEM)
    return pl.pallas_call(
        cross_kernel,
        out_shape=jax.ShapeDtypeStruct(
            (copies, 2 * pair_total, width * width // 2), jnp.bfloat16
        ),
        in_specs=[pl.BlockSpec(memory_space=pltpu.SMEM), vmem, vmem, vmem],
        out_specs=vmem,
        scratch_shapes=[block_rows(pair_total, width)],
        compiler_params=pltpu.CompilerParams(vmem_limit_bytes=VMEM_LIMIT),
        cost_estimate=pl.CostEstimate(flops=2**27, bytes_accessed=2**21, transcendentals=0),
        name="cross_blocks",
    )(plan, own_part, far_basis, stiffness)


ORDER = [5, 4, 6, 3, 7, 2, 0, 1]


def rows_copy(held_ref, out_ref, sems, g):
    pair_total = held_ref.shape[1]
    first = ORDER[g] * pair_total
    return pltpu.make_async_copy(
        held_ref.at[g], out_ref.at[pl.ds(first, pair_total), :], sems.at[g]
    )


LANES = 4


def turn_kernel(flat_ref, out_ref, held_ref, sems, *scratch):
    group_total, pair_total, _ = held_ref.shape
    width = scratch[0].shape[1] // 2
    half = width // 4
    row_at = lax.broadcasted_iota(jnp.int32, (width, 2 * width), 0)
    lane_at = lax.broadcasted_iota(jnp.int32, (width, 2 * width), 1)
    pick = (row_at == lane_at).astype(jnp.bfloat16)

    for g in range(group_total):
        split_ref, rows_ref = scratch[2 * (g % LANES) : 2 * (g % LANES) + 2]
        for k in range(half):
            both = flat_ref[g, :, 2 * width * k : 2 * width * (k + 1)].astype(jnp.float32)
            for at, part in ((k, both[:pair_total]), (k + half, both[pair_total:])):
                split_ref[pl.ds(2 * at, 8, stride=PITCH), :] = part
                split_ref[pl.ds(2 * at + 1, 8, stride=PITCH), :] = pltpu.roll(part, width, 1)
        for p in range(pair_total):
            here = slice(p * PITCH, p * PITCH + width)
            matrix = split_ref[here, :].astype(jnp.bfloat16)
            rows_ref[here, :] = lax.dot_general(
                pick,
                jnp.concatenate([matrix, matrix], axis=0),
                NT,
                preferred_element_type=jnp.float32,
            )
        for k in range(width // 2):
            row = flat_row(rows_ref, width, k)
            held_ref[g, :, 2 * width * k : 2 * width * (k + 1)] = row
        rows_copy(held_ref, out_ref, sems, g).start()

    for g in range(group_total):
        rows_copy(held_ref, out_ref, sems, g).wait()


def widen_kernel(flat_ref, out_ref, held_ref, sems):
    group_total, pair_total, flat_width = held_ref.shape
    for g in range(group_total):
        wide = flat_ref[g].astype(jnp.float32)
        held_ref[g, :, : flat_width // 2] = wide[:pair_total]
        held_ref[g, :, flat_width // 2 :] = wide[pair_total:]
        rows_copy(held_ref, out_ref, sems, g).start()
    for g in range(group_total):
        rows_copy(held_ref, out_ref, sems, g).wait()


def spread(kernel, name, flat, scratch):
    group_total, pair_total, flat_width = flat.shape[0], flat.shape[1] // 2, 2 * flat.shape[2]
    return pl.pallas_call(
        kernel,
        out_shape=jax.ShapeDtypeStruct((group_total * pair_total, flat_width), jnp.float32),
        in_specs=[pl.BlockSpec(memory_space=pltpu.VMEM)],
        out_specs=pl.BlockSpec(memory_space=pl.ANY),
        scratch_shapes=[
            pltpu.VMEM((group_total, pair_total, flat_width), jnp.float32),
            pltpu.SemaphoreType.DMA((group_total,)),
            *scratch,
        ],
        compiler_params=pltpu.CompilerParams(vmem_limit_bytes=VMEM_LIMIT),
        cost_estimate=pl.CostEstimate(flops=2**27, bytes_accessed=2**21, transcendentals=0),
        name=name,
    )(flat)


def on_device(basis, stiffness, pair_subs, own_rows, far_rows, pair_count):
    width = basis.shape[1]
    pair_total, tile_count = own_rows.shape
    far_basis = shifted(basis, "sub", 1)
    plan = planned(pair_subs, own_rows, far_rows, pair_count)
    own_part = collect(plan, basis, tile_count)
    flipped = cross_blocks(plan, own_part, far_basis, stiffness, lax.axis_size("grp"))
    gathered = lax.all_to_all(flipped, "grp", 0, 0, axis_index_groups=[ORDER])
    returned = shifted(gathered, "sub", -1)
    block_scratch = [block_rows(pair_total, width)] * (2 * LANES)
    owned_all = spread(turn_kernel, "turned", gathered, block_scratch)
    partner_all = spread(widen_kernel, "widened", returned, [])
    return (owned_all, partner_all)


def solution(mesh):
    return jax.shard_map(
        on_device,
        mesh=mesh,
        in_specs=(
            P(("sub", "grp"), None, None),
            P(("sub", "grp"), None, None, None),
            P(("sub", "grp"), None),
            P(("sub", "grp"), None),
            P(("sub", "grp"), None),
            P(("sub", "grp")),
        ),
        out_specs=(P("sub", None), P("sub", None)),
        check_vma=False,
    )
```

```python
import jax
import jax.numpy as jnp
from jax import lax
from jax.experimental import pallas as pl
from jax.experimental.pallas import tpu as pltpu
from jax.sharding import PartitionSpec as P

VMEM_LIMIT = 16 * 1024 * 1024


def shifted(block, axis, distance):
    devices = range(lax.axis_size(axis))
    route = [((i - distance) % len(devices), i) for i in devices]
    return lax.ppermute(block, axis, route)


NT = (((1,), (1,)), ((), ()))
PITCH = 72


def block_rows(pair_total, width):
    return pltpu.VMEM(((pair_total + 1) * PITCH, 2 * width), jnp.float32)


def flat_row(rows_ref, width, k):
    left = lax.broadcasted_iota(jnp.int32, (8, 2 * width), 1) < width
    even = rows_ref[pl.ds(2 * k, 8, stride=PITCH), :]
    odd = rows_ref[pl.ds(2 * k + 1, 8, stride=PITCH), :]
    return jnp.where(left, even, odd)


OWN_SUB, FAR_SUB, OWN_TILES, FAR_TILES, LIVE = 0, 1, 2, 6, 10
PAIRS = 8


def planned(pair_subs, own_rows, far_rows, pair_count):
    pair_total = own_rows.shape[0]
    live = jnp.broadcast_to(pair_count[:, None], (1, pair_total))
    return jnp.concatenate([pair_subs.T, own_rows.T, far_rows.T, live], axis=0).reshape(-1)


def tile(basis_ref, plan_ref, sub_at, tile_at, p):
    first = pl.multiple_of(plan_ref[tile_at * PAIRS + p] * 128, 128)
    return basis_ref[plan_ref[sub_at * PAIRS + p], :, pl.ds(first, 128)]


def collect_kernel(plan_ref, basis_ref, part_ref):
    pair_total, _, margin = part_ref.shape
    for p in range(pair_total):
        for t in range(margin // 128):
            part_ref[p, :, t * 128 : (t + 1) * 128] = tile(
                basis_ref, plan_ref, OWN_SUB, OWN_TILES + t, p
            )


def collect(plan, basis, tile_count):
    vmem = pl.BlockSpec(memory_space=pltpu.VMEM)
    shape = (PAIRS, basis.shape[1], tile_count * 128)
    return pl.pallas_call(
        collect_kernel,
        out_shape=jax.ShapeDtypeStruct(shape, basis.dtype),
        in_specs=[pl.BlockSpec(memory_space=pltpu.SMEM), vmem],
        out_specs=vmem,
        compiler_params=pltpu.CompilerParams(vmem_limit_bytes=VMEM_LIMIT),
        cost_estimate=pl.CostEstimate(flops=2**27, bytes_accessed=2**22, transcendentals=0),
        name="collect",
    )(plan, basis)


def cross_kernel(plan_ref, own_ref, far_ref, stiff_ref, out_ref, rows_ref):
    pair_total, tile_count = stiff_ref.shape[:2]
    width = far_ref.shape[1]

    def imaged(p):
        return jnp.concatenate(
            [
                lax.dot_general(
                    tile(far_ref, plan_ref, FAR_SUB, FAR_TILES + t, p),
                    stiff_ref[p, t],
                    NT,
                    preferred_element_type=jnp.float32,
                ).astype(jnp.bfloat16)
                for t in range(tile_count)
            ],
            axis=1,
        )

    def crossed(p, image):
        flipped = lax.dot_general(image, own_ref[p], NT, preferred_element_type=jnp.float32)
        flipped = jnp.concatenate([flipped, flipped], axis=1)
        keep = p < plan_ref[LIVE * PAIRS + p]
        rows_ref[p * PITCH : p * PITCH + width, :] = jnp.where(keep, flipped, 0.0)

    image = imaged(0)
    for p in range(pair_total):
        later = imaged(p + 1) if p + 1 < pair_total else None
        crossed(p, image)
        image = later
    half = width // 4
    for k in range(half):
        both = [flat_row(rows_ref, width, k), flat_row(rows_ref, width, k + half)]
        row = jnp.concatenate(both, axis=0).astype(out_ref.dtype)
        for d in range(out_ref.shape[0]):
            out_ref[d, :, 2 * width * k : 2 * width * (k + 1)] = row


def cross_blocks(plan, own_part, far_basis, stiffness, copies):
    pair_total, width, _ = own_part.shape
    vmem = pl.BlockSpec(memory_space=pltpu.VMEM)
    return pl.pallas_call(
        cross_kernel,
        out_shape=jax.ShapeDtypeStruct(
            (copies, 2 * pair_total, width * width // 2), jnp.bfloat16
        ),
        in_specs=[pl.BlockSpec(memory_space=pltpu.SMEM), vmem, vmem, vmem],
        out_specs=vmem,
        scratch_shapes=[block_rows(pair_total, width)],
        compiler_params=pltpu.CompilerParams(vmem_limit_bytes=VMEM_LIMIT),
        cost_estimate=pl.CostEstimate(flops=2**27, bytes_accessed=2**21, transcendentals=0),
        name="cross_blocks",
    )(plan, own_part, far_basis, stiffness)


ORDER = [5, 4, 6, 3, 7, 2, 0, 1]


def rows_copy(held_ref, out_ref, sems, g):
    pair_total = held_ref.shape[1]
    first = ORDER[g] * pair_total
    return pltpu.make_async_copy(
        held_ref.at[g], out_ref.at[pl.ds(first, pair_total), :], sems.at[g]
    )


LANES = 4


def turn_kernel(flat_ref, out_ref, held_ref, sems, *scratch):
    group_total, pair_total, _ = held_ref.shape
    width = scratch[0].shape[1] // 2
    half = width // 4
    row_at = lax.broadcasted_iota(jnp.int32, (width, 2 * width), 0)
    lane_at = lax.broadcasted_iota(jnp.int32, (width, 2 * width), 1)
    pick = (row_at == lane_at).astype(jnp.bfloat16)

    for g in range(group_total):
        split_ref, rows_ref = scratch[2 * (g % LANES) : 2 * (g % LANES) + 2]
        for k in range(half):
            both = flat_ref[g, :, 2 * width * k : 2 * width * (k + 1)].astype(jnp.float32)
            for at, part in ((k, both[:pair_total]), (k + half, both[pair_total:])):
                split_ref[pl.ds(2 * at, 8, stride=PITCH), :] = part
                split_ref[pl.ds(2 * at + 1, 8, stride=PITCH), :] = pltpu.roll(part, width, 1)
        for p in range(pair_total):
            here = slice(p * PITCH, p * PITCH + width)
            matrix = split_ref[here, :].astype(jnp.bfloat16)
            rows_ref[here, :] = lax.dot_general(
                pick,
                jnp.concatenate([matrix, matrix], axis=0),
                NT,
                preferred_element_type=jnp.float32,
            )
        for k in range(width // 2):
            row = flat_row(rows_ref, width, k)
            held_ref[g, :, 2 * width * k : 2 * width * (k + 1)] = row
        rows_copy(held_ref, out_ref, sems, g).start()

    for g in range(group_total):
        rows_copy(held_ref, out_ref, sems, g).wait()


def widen_kernel(flat_ref, out_ref, held_ref, sems):
    group_total, pair_total, flat_width = held_ref.shape
    for g in range(group_total):
        wide = flat_ref[g].astype(jnp.float32)
        held_ref[g, :, : flat_width // 2] = wide[:pair_total]
        held_ref[g, :, flat_width // 2 :] = wide[pair_total:]
        rows_copy(held_ref, out_ref, sems, g).start()
    for g in range(group_total):
        rows_copy(held_ref, out_ref, sems, g).wait()


def spread(kernel, name, flat, scratch):
    group_total, pair_total, flat_width = flat.shape[0], flat.shape[1] // 2, 2 * flat.shape[2]
    return pl.pallas_call(
        kernel,
        out_shape=jax.ShapeDtypeStruct((group_total * pair_total, flat_width), jnp.float32),
        in_specs=[pl.BlockSpec(memory_space=pltpu.VMEM)],
        out_specs=pl.BlockSpec(memory_space=pl.ANY),
        scratch_shapes=[
            pltpu.VMEM((group_total, pair_total, flat_width), jnp.float32),
            pltpu.SemaphoreType.DMA((group_total,)),
            *scratch,
        ],
        compiler_params=pltpu.CompilerParams(vmem_limit_bytes=VMEM_LIMIT),
        cost_estimate=pl.CostEstimate(flops=2**27, bytes_accessed=2**21, transcendentals=0),
        name=name,
    )(flat)


def on_device(basis, stiffness, pair_subs, own_rows, far_rows, pair_count):
    width = basis.shape[1]
    pair_total, tile_count = own_rows.shape
    far_basis = shifted(basis, "sub", 1)
    plan = planned(pair_subs, own_rows, far_rows, pair_count)
    own_part = collect(plan, basis, tile_count)
    flipped = cross_blocks(plan, own_part, far_basis, stiffness, lax.axis_size("grp"))
    gathered = lax.all_to_all(flipped, "grp", 0, 0, axis_index_groups=[ORDER])
    returned = shifted(gathered, "sub", -1)
    block_scratch = [block_rows(pair_total, width)] * (2 * LANES)
    owned_all = spread(turn_kernel, "turned", gathered, block_scratch)
    partner_all = spread(widen_kernel, "widened", returned, [])
    return (owned_all, partner_all)


def solution(mesh):
    return jax.shard_map(
        on_device,
        mesh=mesh,
        in_specs=(
            P(("sub", "grp"), None, None),
            P(("sub", "grp"), None, None, None),
            P(("sub", "grp"), None),
            P(("sub", "grp"), None),
            P(("sub", "grp"), None),
            P(("sub", "grp")),
        ),
        out_specs=(P("sub", None), P("sub", None)),
        check_vma=False,
    )
```
